32 devices in a mesh: det: 8 (over z, x), tm: 4 (over y, core).
Axes of the slice: x: 2, y: 2, z: 4, core: 2. Of those that a mesh axis runs over, the one named last changes fastest.
Arguments:
- x_map: float32 [3, 4096, 256], P(None, ('det', 'tm')), may hold values from -6 to 6
- r_map: float32 [3, 4096, 256], P(None, ('det', 'tm')), may hold values from -45 to 45
- p_map: float32 [3, 4096, 256], P(None, ('det', 'tm')), may hold values from -45 to 45
- pointing: int32 [32, 16384], P('det', 'tm'), may hold values from 0 to 2047
- pol_angle: float32 [32, 16384], P('det', 'tm'), may hold values from -3.140625 to 3.140625
- noise_filter: bfloat16 [32, 8192], P('det'), may hold values from -2 to 2
- block_list: int32 [8, 128, 8], P('det', 'tm'), may hold values from 0 to 4095, as said below
- block_home: int32 [4096], replicated, may hold values from 0 to 4095, as said below
Outputs:
- x_next: float32 [3, 4096, 256], P(None, ('det', 'tm'))
- r_next: float32 [3, 4096, 256], P(None, ('det', 'tm'))
- p_next: float32 [3, 4096, 256], P(None, ('det', 'tm'))
The draws below stay inside these ranges and needn't reach their ends.
Inputs may be any that keep to these rules, and one draw needn't show every extreme that they name: Block b is stored at row block_home[b] of the maps, a permutation. `block_list`: repeats allowed. The 256 entries of one device's lists name at most 16 blocks stored on any one device (counted with repeats), exactly 16 on some; one device's stored blocks are named 16 times by every device's lists.
All inputs are finite; a program needn't handle non-finite values.
Results may differ from the reference program's by a relative error of at most 0.0034.
The reference program's roundings to bfloat16 on the way (of `signal` and `filtered`) count: a program that leaves them out, or rounds other values in their place, can miss the bound.
Values may be sent and summed in bfloat16 or wider, within the bound.
A program may use at most 128 MiB of HBM per device.

```python
import math
import jax
import jax.numpy as jnp
from jax import lax

DET_DEV = 4
BLOCKS_DEV = 128
TAPS = 8192
PIXELS = 256
TBLOCKS = 32
LIST = 8
SPAN = 128
HITS = 1
DETECTORS = 32
TIME = 16384
MAP_BLOCKS = 4096
N_DET = 8
N_TM = 4


def field_draw(key, salt):
    base_key = jax.random.fold_in(key, salt)
    noise_key, scale_key = jax.random.split(base_key)
    shape = (3, MAP_BLOCKS, PIXELS)
    rising = 3.0 ** (jnp.arange(MAP_BLOCKS, dtype=jnp.float32) / MAP_BLOCKS)
    spread = jnp.exp(jax.random.uniform(scale_key, (3, MAP_BLOCKS, 1), jnp.float32, math.log(0.3), math.log(3.0)))
    values = jnp.clip(jax.random.normal(noise_key, shape, jnp.float32), -4.5, 4.5) + 0.5
    return values * spread * rising[None, :, None]


def draw_r_map(key, part):
    return field_draw(key, 21)


def draw_p_map(key, part):
    return field_draw(key, 22)


def draw_noise_filter(key, part):
    weight_key, tap_key = jax.random.split(jax.random.fold_in(key, 31))
    weight = jnp.exp(jax.random.uniform(weight_key, (DETECTORS, 1), jnp.float32, math.log(0.5), math.log(2.0))) / HITS
    distance = jnp.abs(jnp.arange(TAPS, dtype=jnp.int32) - TAPS // 2).astype(jnp.float32)
    uneven = jnp.clip(0.5 * jax.random.normal(tap_key, (DETECTORS, TAPS), jnp.float32), -1.0, 1.0)
    reach = jnp.maximum(distance, 1.0)[None, :]
    nearest = -0.1 * (1.0 + 0.5 * uneven)
    coherent = -0.35 / (4.0 * math.sqrt(TAPS // 2)) / jnp.sqrt(reach)
    distant = 0.1 * uneven / (2.0 * math.log(TAPS) * reach) + coherent
    taps_all = jnp.where(distance[None, :] == 0.0, 1.0, jnp.where(distance[None, :] == 1.0, nearest, distant))
    return (weight * taps_all).astype(jnp.bfloat16)


def home_table(key):
    return jax.random.permutation(jax.random.fold_in(key, 41), MAP_BLOCKS).astype(jnp.int32)


def draw_block_home(key, part):
    return home_table(key)


def draw_block_list(key, part):
    devices = N_DET * N_TM
    entries = TBLOCKS * LIST
    mean_load = entries // devices
    quarter = devices // 4
    inverse = jnp.argsort(home_table(key)).astype(jnp.int32)
    hottest = jax.random.randint(jax.random.fold_in(key, 42), (), 0, devices)
    rank_keys = jax.random.split(jax.random.fold_in(key, 43), devices)
    ranking = jax.vmap(lambda one_key: jax.random.permutation(one_key, devices))(rank_keys).astype(jnp.int32)
    hot_rank = ranking[:, hottest]
    column = jnp.arange(devices, dtype=jnp.int32)
    ranking = jnp.where(column[None, :] == hottest, 0, jnp.where(ranking == 0, hot_rank[:, None], ranking))
    loads = jnp.where(ranking < quarter, 2 * mean_load, jnp.where(ranking < 2 * quarter, 3 * mean_load // 2, jnp.where(ranking < 3 * quarter, mean_load // 2, 0)))
    bounds = jnp.cumsum(loads, axis=1)
    entry_index = jnp.arange(entries, dtype=jnp.int32)
    owners = jnp.sum((bounds[:, None, :] <= entry_index[None, :, None]).astype(jnp.int32), axis=2)
    mix_keys = jax.random.split(jax.random.fold_in(key, 44), devices)
    order = jax.vmap(lambda one_key: jax.random.permutation(one_key, entries))(mix_keys)
    owners = jnp.take_along_axis(owners, order, axis=1)
    slot_draw = jax.random.randint(jax.random.fold_in(key, 45), (devices, entries), 0, BLOCKS_DEV)
    chosen = inverse[owners * BLOCKS_DEV + slot_draw]
    return chosen.reshape(N_DET, N_TM * TBLOCKS, LIST).astype(jnp.int32)


def plant(drawn, stream_key, smallest, largest):
    spot = [jax.random.randint(jax.random.fold_in(stream_key, axis), (), 0, length) for axis, length in enumerate(drawn.shape)]
    longest = drawn.shape.index(max(drawn.shape))
    next_to = spot[:longest] + [(spot[longest] + 1) % drawn.shape[longest]] + spot[longest + 1:]
    return drawn.at[tuple(spot)].set(smallest).at[tuple(next_to)].set(largest)


def shard_levels(rng, shape, cuts, least, high):
    def one(dim, shards_of):
        steps = jax.random.uniform(jax.random.fold_in(jax.random.fold_in(rng, 6), dim), (shards_of,), jnp.float32, least / len(cuts), high / len(cuts))
        return jnp.repeat(jnp.exp(steps), shape[dim] // shards_of).reshape((-1,) + (1,) * (len(shape) - dim - 1))

    loudness = one(*cuts[0])
    for cut in cuts[1:]:
        loudness = loudness * one(*cut)
    return loudness


def bell_draw(own_key, shape, width, limit, cuts=(), kind=jnp.bfloat16):
    values = jax.random.normal(own_key, shape, jnp.float32) * width
    if len(cuts) > 0:
        values = shard_levels(own_key, shape, cuts, -0.22, 0.18) * values
    return jnp.clip(values, min=-limit, max=limit).astype(kind)


def setup_inputs(seed: int = 0) -> dict:
    keys = jax.random.split(jax.random.key(seed), 9)
    x_map = bell_draw(keys[0], (3, MAP_BLOCKS, PIXELS), 1.0, 6.0, ((1, 32),), jnp.float32)
    r_map = draw_r_map(jax.random.fold_in(keys[8], 71), 0)
    p_map = draw_p_map(jax.random.fold_in(keys[8], 71), 0)
    pointing = plant(jax.random.randint(keys[3], (DETECTORS, TIME), 0, LIST * PIXELS), jax.random.fold_in(keys[3], 1), 0, (LIST * PIXELS) - 1).astype(jnp.int32)
    pol_angle = jnp.clip(jax.random.uniform(keys[4], (DETECTORS, TIME), jnp.float32, -3.140625, 3.140625), -3.140625, 3.140625)
    noise_filter = draw_noise_filter(jax.random.fold_in(keys[8], 71), 0)
    block_list = draw_block_list(jax.random.fold_in(keys[8], 71), 0)
    block_home = draw_block_home(jax.random.fold_in(keys[8], 71), 0)
    return dict(x_map=x_map, r_map=r_map, p_map=p_map, pointing=pointing, pol_angle=pol_angle, noise_filter=noise_filter, block_list=block_list, block_home=block_home)


def filter_group(signal, coeffs):
    series = signal.astype(jnp.float32)
    kernel = coeffs.astype(jnp.float32)[:, ::-1]
    length = TIME + TAPS
    fft_len = 1 << (length - 1).bit_length()
    spectrum = jnp.fft.rfft(series, fft_len, axis=1) * jnp.fft.rfft(kernel, fft_len, axis=1)
    convolved = jnp.fft.irfft(spectrum, fft_len, axis=1)
    return convolved[:, TAPS // 2 - 1:TAPS // 2 - 1 + TIME]


def reference(x_map, r_map, p_map, pointing, pol_angle, noise_filter, block_list, block_home):
    by_block = p_map[:, block_home, :].reshape(3, MAP_BLOCKS * PIXELS)
    time_block = jnp.arange(TIME, dtype=jnp.int32) // SPAN

    def per_group(image, index):
        start = index * DET_DEV
        aim = lax.dynamic_slice_in_dim(pointing, start, DET_DEV, 0)
        angle_rows = lax.dynamic_slice_in_dim(pol_angle, start, DET_DEV, 0)
        coeffs = lax.dynamic_slice_in_dim(noise_filter, start, DET_DEV, 0)
        lists = block_list[index]
        chosen = lists[time_block[None, :], aim // PIXELS]
        address = (chosen * PIXELS + aim % PIXELS).astype(jnp.int32)
        cosine = jnp.cos(2.0 * angle_rows)
        sine_part = jnp.sin(2.0 * angle_rows)
        signal = (by_block[0][address] + cosine * by_block[1][address] + sine_part * by_block[2][address]).astype(jnp.bfloat16)
        rounded = filter_group(signal, coeffs).astype(jnp.bfloat16)
        filtered = lax.optimization_barrier(rounded).astype(jnp.float32)
        terms = jnp.stack([filtered, filtered * cosine, filtered * sine_part]).reshape(3, -1)
        image = image.at[:, address.reshape(-1)].add(terms)
        return image, None

    image_ids, unused = lax.scan(per_group, jnp.zeros((3, MAP_BLOCKS * PIXELS), jnp.float32), jnp.arange(N_DET, dtype=jnp.int32))
    image = jnp.zeros_like(p_map).at[:, block_home, :].set(image_ids.reshape(3, MAP_BLOCKS, PIXELS))
    norm_old = jnp.sum(r_map * r_map)
    curvature = jnp.sum(p_map * image)
    step_size = norm_old / curvature
    x_next = x_map + step_size * p_map
    r_next = r_map - step_size * image
    norm_new = jnp.sum(r_next * r_next)
    p_next = r_next + (norm_new / norm_old) * p_map
    return x_next, r_next, p_next
```

```python
import functools

import jax
import jax.numpy as jnp
from jax import lax
from jax.experimental import pallas as pl
from jax.experimental.pallas import tpu as pltpu
from jax.sharding import PartitionSpec as P

F32 = jnp.float32
BF16 = jnp.bfloat16
NN = (((1,), (0,)), ((), ()))
NT = (((1,), (1,)), ((), ()))
TN = (((0,), (0,)), ((), ()))


def dot(a, b, dims):
    return lax.dot_general(a, b, dims, preferred_element_type=F32)


def iota(shape, dim):
    return lax.broadcasted_iota(jnp.int32, shape, dim)


def onehot(cond):
    return jnp.where(cond, 1.0, 0.0).astype(BF16)


def quantize(value):
    largest = jnp.max(jnp.abs(value), axis=1, keepdims=True)
    exponent = jnp.ceil(jnp.log2(jnp.clip(largest, 1e-30, 1e30)))
    whole = jnp.clip(jnp.round(value * jnp.exp2(15.0 - exponent)), -32767.0, 32767.0)
    high = jnp.floor(whole * (1.0 / 256.0))
    return high.astype(BF16), (whole - 256.0 * high).astype(BF16), exponent


def split(words):
    whole = words.astype(jnp.int32).astype(F32)
    high = jnp.floor(whole * (1.0 / 256.0))
    return high, whole - 256.0 * high


def exponent_lanes(exponents):
    rows = exponents[0].shape[0]
    lane = iota((rows, 128), 1)
    out = jnp.zeros((rows, 128), F32)
    for c, e in enumerate(exponents):
        out = jnp.where(lane == c, e, out)
    return out.astype(BF16)


def kernel(
    n_det, n_tm, cap,
    x_ref, r_ref, p_ref, point_ref, angle_ref, filter_ref, wanted_ref, home_ref,
    xo_ref, ro_ref, po_ref,
    ask_out, ask_in, ans_out, ans_in, ret_out, ret_in, red_out, red_in,
    place_ref, hot_ref, toep_ref, frames_ref, pt_ref, cos_ref, sin_ref, sig_ref, y_ref,
    series_ref, halo_out, halo_low, halo_high, lmh_ref, lml_ref, part_ref, image_ref,
    send_sem, recv_sem, halo_send, halo_recv,
):
    n = n_det * n_tm
    det, tm = lax.axis_index("det"), lax.axis_index("tm")
    me = det * n_tm + tm
    comps, blocks, pixels = p_ref.shape
    dets, samples = point_ref.shape
    entries = wanted_ref.shape[1]
    slots = n * cap
    tblocks = samples // 128
    per_block = entries // tblocks
    taps = filter_ref.shape[1]
    tap_rows = taps // 128
    wide = dets * 128
    data = comps * pixels

    def device(index):
        return (index // n_tm, index % n_tm)

    barrier = pltpu.get_barrier_semaphore()

    def greet(k, c):
        pl.semaphore_signal(
            barrier, inc=1, device_id=device((me + k) % n), device_id_type=pl.DeviceIdType.MESH
        )
        return c

    lax.fori_loop(1, n, greet, 0)

    def send_copy(stage, out, into, peer):
        return pltpu.make_async_remote_copy(
            src_ref=out, dst_ref=into.at[me], send_sem=send_sem.at[stage, peer],
            recv_sem=recv_sem.at[stage, me], device_id=device(peer),
            device_id_type=pl.DeviceIdType.MESH,
        )

    def recv_copy(stage, out, into, peer):
        return pltpu.make_async_remote_copy(
            src_ref=out, dst_ref=into.at[peer], send_sem=send_sem.at[stage, peer],
            recv_sem=recv_sem.at[stage, peer], device_id=device(peer),
            device_id_type=pl.DeviceIdType.MESH,
        )

    def send_all(stage, source, into):
        def step(k, c):
            peer = (me + k) % n
            send_copy(stage, source(peer), into, peer).start()
            return c

        lax.fori_loop(1, n, step, 0)

    def wait_all(stage, source, into):
        def step(k, c):
            peer = (me + n - k) % n
            recv_copy(stage, source(peer), into, peer).wait_recv()
            return c

        lax.fori_loop(1, n, step, 0)

    def wait_sent(stage, source, into):
        def step(k, c):
            peer = (me + k) % n
            send_copy(stage, source(peer), into, peer).wait_send()
            return c

        lax.fori_loop(1, n, step, 0)

    wanted = wanted_ref[...]
    home = home_ref[...]
    home_rows = home.shape[0]
    low_hot = onehot(iota((128, entries), 0) == (wanted & 127))
    row_mask = iota((home_rows, entries), 0) == (wanted >> 7)
    owner_table = (home // blocks).astype(F32).astype(BF16)
    slot_table = (home % blocks).astype(F32).astype(BF16)

    def lookup(table):
        return jnp.sum(jnp.where(row_mask, dot(table, low_hot, NN), 0.0), axis=0, keepdims=True)

    owner = lookup(owner_table).astype(jnp.int32)
    slot = lookup(slot_table).astype(jnp.int32)
    member = iota((n, entries), 0) == owner
    earlier = onehot(iota((entries, entries), 0) < iota((entries, entries), 1))
    rank = jnp.sum(
        jnp.where(member, dot(onehot(member), earlier, NN), 0.0), axis=0, keepdims=True
    ).astype(jnp.int32)
    place_ref[...] = onehot(iota((slots, entries), 0) == owner * cap + rank)
    slot_hot = onehot(iota((blocks, entries), 0) == slot)
    ask_out[...] = dot(place_ref[...], slot_hot, NT).astype(BF16).reshape(n, cap, blocks)
    pl.semaphore_wait(barrier, n - 1)
    send_all(0, lambda d: ask_out.at[d], ask_in)
    ask_in[pl.ds(me, 1)] = ask_out[pl.ds(me, 1)]

    pieces = [quantize(p_ref[c]) for c in range(comps)]
    scales = exponent_lanes([e for _, _, e in pieces])

    wait_all(0, lambda d: ask_out.at[d], ask_in)
    asked = ask_in[...].reshape(slots, blocks)

    def place_words(selector, high, low):
        return (256.0 * dot(selector, high, NN) + dot(selector, low, NN)).astype(jnp.int32)

    def fill(buffer, selector, quantized, scale_lanes):
        for c, (high, low, _) in enumerate(quantized):
            words = place_words(selector, high, low).astype(jnp.int16)
            buffer[:, :, c * pixels : (c + 1) * pixels] = words.reshape(n, cap, pixels)
        words = dot(selector, scale_lanes, NN).astype(jnp.int32).astype(jnp.int16)
        buffer[:, :, data : data + 128] = words.reshape(n, cap, 128)

    fill(ans_out, asked, pieces, scales)
    send_all(1, lambda d: ans_out.at[d], ans_in)
    ans_in[pl.ds(me, 1)] = ans_out[pl.ds(me, 1)]

    for b in range(tblocks):
        for d in range(dets):
            here = slice(d * 128, (d + 1) * 128)
            pt_ref[b : b + 1, here] = point_ref[d : d + 1, b * 128 : (b + 1) * 128]
            cos_ref[b : b + 1, here] = angle_ref[d : d + 1, b * 128 : (b + 1) * 128]
    twice = 2.0 * cos_ref[...]
    cos_ref[...] = jnp.cos(twice)
    sin_ref[...] = jnp.sin(twice)

    def make_hot(b, c):
        pixel = pt_ref[pl.ds(b, 1), :] & (pixels - 1)
        hot_ref[b] = onehot(iota((pixels, wide), 0) == pixel)
        return c

    lax.fori_loop(0, tblocks, make_hot, 0)
    upper = iota((128, 128), 1) >= iota((128, 128), 0)

    def turned(tile):
        full = jnp.broadcast_to(tile.astype(F32), (128, 128))
        return pltpu.roll(full, 0, 1, stride=1, stride_axis=0)

    def make_toeplitz(b, before):
        lanes = pl.ds(pl.multiple_of(b * 128, 128), 128)
        now = []
        taps_here = filter_ref[:, lanes].astype(F32)
        for d in range(dets):
            tile = turned(taps_here[d : d + 1, :])
            toep_ref[d, :, lanes] = jnp.where(upper, tile, before[d]).astype(BF16)
            now.append(tile)
        return tuple(now)

    zero = jnp.zeros((128, 128), F32)
    last = lax.fori_loop(0, tap_rows, make_toeplitz, (zero,) * dets)
    for d in range(dets):
        toep_ref[d, :, taps : taps + 128] = jnp.where(upper, 0.0, last[d]).astype(BF16)

    wait_all(1, lambda d: ans_out.at[d], ans_in)

    words = ans_in[:, :, data : data + 128].reshape(slots, 128)
    place = place_ref[...]
    exps = dot(place, words.astype(jnp.int32).astype(F32).astype(BF16), TN)
    for c in range(comps):
        high, low = split(ans_in[:, :, c * pixels : (c + 1) * pixels].reshape(slots, pixels))
        scale = jnp.exp2(exps[:, c : c + 1] - 15.0)
        lmh_ref[c] = dot(place, high.astype(BF16), TN) * (256.0 * scale)
        lml_ref[c] = dot(place, low.astype(BF16), TN) * scale

    def entry_mask(b):
        return iota((per_block, wide), 0) == (pt_ref[pl.ds(b, 1), :] // pixels)

    def scan_signal(b, carry):
        rows = pl.ds(pl.multiple_of(b * per_block, per_block), per_block)
        table = jnp.concatenate(
            [ref[c, rows, :] for c in range(comps) for ref in (lmh_ref, lml_ref)], axis=0
        ).astype(BF16)
        seen = dot(table, hot_ref[b], NN)
        parts = [
            seen[2 * c * per_block : (2 * c + 1) * per_block]
            + seen[(2 * c + 1) * per_block : (2 * c + 2) * per_block]
            for c in range(comps)
        ]
        value = (
            parts[0] + cos_ref[pl.ds(b, 1), :] * parts[1] + sin_ref[pl.ds(b, 1), :] * parts[2]
        )
        sig_ref[pl.ds(b, 1), :] = jnp.sum(
            jnp.where(entry_mask(b), value, 0.0), axis=0, keepdims=True
        )
        return carry

    lax.fori_loop(0, tblocks, scan_signal, 0, unroll=4)
    halo_out[...] = sig_ref[...].astype(BF16)

    def halo(side, target, buffer):
        return pltpu.make_async_remote_copy(
            src_ref=halo_out, dst_ref=buffer, send_sem=halo_send.at[side],
            recv_sem=halo_recv.at[side], device_id=(det, target),
            device_id_type=pl.DeviceIdType.MESH,
        )

    to_right = halo(0, (tm + 1) % n_tm, halo_low)
    to_left = halo(1, (tm + n_tm - 1) % n_tm, halo_high)

    @pl.when(tm < n_tm - 1)
    def _():
        to_right.start()

    @pl.when(tm > 0)
    def _():
        to_left.start()

    series_ref[tblocks : 2 * tblocks, :] = halo_out[...].astype(F32)

    @pl.when(tm > 0)
    def _():
        to_right.wait_recv()
        series_ref[0:tblocks, :] = halo_low[...].astype(F32)

    @pl.when(tm == 0)
    def _():
        series_ref[0:tblocks, :] = jnp.zeros((tblocks, wide), F32)

    @pl.when(tm < n_tm - 1)
    def _():
        to_left.wait_recv()
        series_ref[2 * tblocks : 3 * tblocks, :] = halo_high[...].astype(F32)

    @pl.when(tm == n_tm - 1)
    def _():
        series_ref[2 * tblocks : 3 * tblocks, :] = jnp.zeros((tblocks, wide), F32)

    def make_frames(group, c):
        near = series_ref[pl.ds(pl.multiple_of(group * 8, 8), tblocks + 8), :]
        for r in range(8):
            rows = near[r : r + tblocks, :].astype(BF16)
            lanes = pl.ds(pl.multiple_of((group * 8 + r) * 128, 128), 128)
            for d in range(dets):
                frames_ref[d, :, lanes] = rows[:, d * 128 : (d + 1) * 128]
        return c

    lax.fori_loop(0, tap_rows // 8, make_frames, 0)
    end = series_ref[2 * tblocks : 3 * tblocks, :].astype(BF16)
    for d in range(dets):
        frames_ref[d, :, taps : taps + 128] = end[:, d * 128 : (d + 1) * 128]
    for d in range(dets):
        y_ref[:, d * 128 : (d + 1) * 128] = (
            dot(frames_ref[d], toep_ref[d], NT).astype(BF16).astype(F32)
        )

    def scan_bins(b, carry):
        rows = pl.ds(pl.multiple_of(b * per_block, per_block), per_block)
        mask = entry_mask(b)
        filtered = y_ref[pl.ds(b, 1), :]
        stack = [jnp.where(mask, filtered, 0.0)]
        for weight in (cos_ref, sin_ref):
            term = jnp.where(mask, filtered * weight[pl.ds(b, 1), :], 0.0)
            high = term.astype(BF16).astype(F32)
            stack += [high, term - high]
        stack.append(jnp.zeros((per_block, wide), F32))
        sums = dot(jnp.concatenate(stack, axis=0).astype(BF16), hot_ref[b], NT)
        g = per_block
        part_ref[0, rows, :] = sums[0:g]
        part_ref[1, rows, :] = sums[g : 2 * g] + sums[2 * g : 3 * g]
        part_ref[2, rows, :] = sums[3 * g : 4 * g] + sums[4 * g : 5 * g]
        return carry

    lax.fori_loop(0, tblocks, scan_bins, 0, unroll=4)

    outgoing = [quantize(part_ref[c]) for c in range(comps)]
    fill(ret_out, place_ref[...], outgoing, exponent_lanes([e for _, _, e in outgoing]))
    send_all(2, lambda d: ret_out.at[d], ret_in)
    ret_in[pl.ds(me, 1)] = ret_out[pl.ds(me, 1)]
    wait_all(2, lambda d: ret_out.at[d], ret_in)

    chosen = ask_in[...].reshape(slots, blocks)
    exps = ret_in[:, :, data : data + 128].reshape(slots, 128).astype(jnp.int32).astype(F32)
    totals = [jnp.zeros((1, 1), F32)] * 4
    for c in range(comps):
        high, low = split(ret_in[:, :, c * pixels : (c + 1) * pixels].reshape(slots, pixels))
        scale = jnp.exp2(exps[:, c : c + 1] - 15.0)
        image = dot(chosen, (high * (256.0 * scale)).astype(BF16), TN) + dot(
            chosen, (low * scale).astype(BF16), TN
        )
        image_ref[c] = image
        residual = r_ref[c]
        for i, product in enumerate(
            (residual * residual, p_ref[c] * image, residual * image, image * image)
        ):
            totals[i] = totals[i] + jnp.sum(product, keepdims=True)
    lane = iota((8, 128), 1)
    packed = jnp.zeros((8, 128), F32)
    for i in range(4):
        packed = jnp.where(lane == i, totals[i], packed)
    red_out[...] = packed
    red_in[pl.ds(me, 1)] = packed.reshape(1, 8, 128)
    send_all(3, lambda d: red_out, red_in)
    wait_all(3, lambda d: red_out, red_in)
    summed = jnp.sum(red_in[...], axis=0)[0:1, :]
    lane = iota((1, 128), 1)
    norm_old, curvature, cross, square = (
        jnp.sum(jnp.where(lane == i, summed, 0.0), axis=1, keepdims=True) for i in range(4)
    )
    step = norm_old / curvature
    norm_new = norm_old - 2.0 * step * cross + step * step * square
    ratio = norm_new / norm_old
    for c in range(comps):
        direction = p_ref[c]
        residual = r_ref[c] - step * image_ref[c]
        xo_ref[c] = x_ref[c] + step * direction
        ro_ref[c] = residual
        po_ref[c] = residual + ratio * direction

    wait_sent(0, lambda d: ask_out.at[d], ask_in)
    wait_sent(1, lambda d: ans_out.at[d], ans_in)
    wait_sent(2, lambda d: ret_out.at[d], ret_in)
    wait_sent(3, lambda d: red_out, red_in)

    @pl.when(tm < n_tm - 1)
    def _():
        to_right.wait_send()

    @pl.when(tm > 0)
    def _():
        to_left.wait_send()


def body(n_det, n_tm, x_map, r_map, p_map, pointing, pol_angle, noise_filter, block_list, block_home):
    n = n_det * n_tm
    comps, blocks, pixels = p_map.shape
    dets, samples = pointing.shape
    tblocks = block_list.shape[1]
    entries = tblocks * block_list.shape[2]
    taps = noise_filter.shape[1]
    cap = -(-(2 * entries // n) // 16) * 16
    slots = n * cap
    wide = dets * 128
    width = comps * pixels + 128
    assert samples == tblocks * 128 and taps == 2 * samples
    vmem = pltpu.VMEM
    out = jax.ShapeDtypeStruct(p_map.shape, F32)
    return pl.pallas_call(
        functools.partial(kernel, n_det, n_tm, cap),
        out_shape=(out, out, out),
        in_specs=[pl.BlockSpec(memory_space=vmem)] * 8,
        out_specs=[pl.BlockSpec(memory_space=vmem)] * 3,
        scratch_shapes=[
            vmem((n, cap, blocks), BF16),
            vmem((n, cap, blocks), BF16),
            vmem((n, cap, width), jnp.int16),
            vmem((n, cap, width), jnp.int16),
            vmem((n, cap, width), jnp.int16),
            vmem((n, cap, width), jnp.int16),
            vmem((8, 128), F32),
            vmem((n, 8, 128), F32),
            vmem((slots, entries), BF16),
            vmem((tblocks, pixels, wide), BF16),
            vmem((dets, 128, taps + 128), BF16),
            vmem((dets, tblocks, taps + 128), BF16),
            vmem((tblocks, wide), jnp.int32),
            vmem((tblocks, wide), F32),
            vmem((tblocks, wide), F32),
            vmem((tblocks, wide), F32),
            vmem((tblocks, wide), F32),
            vmem((3 * tblocks, wide), F32),
            vmem((tblocks, wide), BF16),
            vmem((tblocks, wide), BF16),
            vmem((tblocks, wide), BF16),
            vmem((comps, entries, pixels), F32),
            vmem((comps, entries, pixels), F32),
            vmem((comps, entries, pixels), F32),
            vmem((comps, blocks, pixels), F32),
            pltpu.SemaphoreType.DMA((4, n)),
            pltpu.SemaphoreType.DMA((4, n)),
            pltpu.SemaphoreType.DMA((2,)),
            pltpu.SemaphoreType.DMA((2,)),
        ],
        compiler_params=pltpu.CompilerParams(
            collective_id=0, has_side_effects=True, vmem_limit_bytes=60 * 1024 * 1024
        ),
    )(
        x_map, r_map, p_map, pointing, pol_angle, noise_filter,
        block_list.reshape(1, entries), block_home.reshape(-1, 128),
    )


def solution(mesh):
    maps = P(None, ("det", "tm"), None)
    return jax.shard_map(
        functools.partial(body, mesh.shape["det"], mesh.shape["tm"]),
        mesh=mesh,
        in_specs=(
            maps, maps, maps, P("det", "tm"), P("det", "tm"), P("det", None),
            P("det", "tm", None), P(),
        ),
        out_specs=(maps, maps, maps),
        check_vma=False,
    )
```

```python
import functools

import jax
import jax.numpy as jnp
from jax import lax
from jax.experimental import pallas as pl
from jax.experimental.pallas import tpu as pltpu
from jax.sharding import PartitionSpec as P

F32 = jnp.float32
BF16 = jnp.bfloat16
NN = (((1,), (0,)), ((), ()))
NT = (((1,), (1,)), ((), ()))
TN = (((0,), (0,)), ((), ()))


def dot(a, b, dims):
    return lax.dot_general(a, b, dims, preferred_element_type=F32)


def iota(shape, dim):
    return lax.broadcasted_iota(jnp.int32, shape, dim)


def onehot(cond):
    return jnp.where(cond, 1.0, 0.0).astype(BF16)


def quantize(value):
    largest = jnp.max(jnp.abs(value), axis=1, keepdims=True)
    exponent = jnp.ceil(jnp.log2(jnp.clip(largest, 1e-30, 1e30)))
    whole = jnp.clip(jnp.round(value * jnp.exp2(15.0 - exponent)), -32767.0, 32767.0)
    high = jnp.floor(whole * (1.0 / 256.0))
    return high.astype(BF16), (whole - 256.0 * high).astype(BF16), exponent


def split(words):
    whole = words.astype(jnp.int32).astype(F32)
    high = jnp.floor(whole * (1.0 / 256.0))
    return high, whole - 256.0 * high


def exponent_lanes(exponents):
    rows = exponents[0].shape[0]
    lane = iota((rows, 128), 1)
    out = jnp.zeros((rows, 128), F32)
    for c, e in enumerate(exponents):
        out = jnp.where(lane == c, e, out)
    return out.astype(BF16)


def kernel(
    n_det, n_tm, cap,
    x_ref, r_ref, p_ref, point_ref, angle_ref, filter_ref, wanted_ref, home_ref,
    xo_ref, ro_ref, po_ref,
    ask_out, ask_in, ans_out, ans_in, ret_out, ret_in, red_out, red_in,
    ans_scale_out, ans_scale_in, ret_scale_out, ret_scale_in,
    place_ref, hot_ref, toep_ref, frames_ref, pt_ref, cos_ref, sin_ref, sig_ref, y_ref,
    series_ref, halo_out, halo_low, halo_high, lmh_ref, lml_ref, part_ref, image_ref,
    send_sem, recv_sem, red_send, red_recv, halo_send, halo_recv,
):
    n = n_det * n_tm
    det, tm = lax.axis_index("det"), lax.axis_index("tm")
    me = det * n_tm + tm
    comps, blocks, pixels = p_ref.shape
    dets, samples = point_ref.shape
    entries = wanted_ref.shape[1]
    slots = n * cap
    tblocks = samples // 128
    per_block = entries // tblocks
    taps = filter_ref.shape[1]
    tap_rows = taps // 128
    half = n // 2
    wide = dets * 128

    def device(index):
        return (index // n_tm, index % n_tm)

    barrier = pltpu.get_barrier_semaphore()

    def greet(k, c):
        pl.semaphore_signal(
            barrier, inc=1, device_id=device((me + k) % n), device_id_type=pl.DeviceIdType.MESH
        )
        return c

    lax.fori_loop(1, n, greet, 0)

    def send_all(*sends):
        def start(peer):
            for stage, source, into in sends:
                pltpu.make_async_remote_copy(
                    src_ref=source(peer), dst_ref=into.at[me], send_sem=send_sem.at[stage],
                    recv_sem=recv_sem.at[stage], device_id=device(peer),
                    device_id_type=pl.DeviceIdType.MESH,
                ).start()

        mine = (me // half) * half

        def far(k, c):
            start((mine + half) % n + (me + k) % half)
            return c

        def near(k, c):
            start(mine + (me + k) % half)
            return c

        lax.fori_loop(0, half, far, 0)
        lax.fori_loop(1, half, near, 0)

    def everything(stage, buffer):
        whole = buffer.at[pl.ds(0, n - 1)]
        return pltpu.make_async_remote_copy(
            src_ref=whole, dst_ref=whole, send_sem=send_sem.at[stage],
            recv_sem=recv_sem.at[stage], device_id=device((me + 1) % n),
            device_id_type=pl.DeviceIdType.MESH,
        )

    wanted = wanted_ref[...]
    home = home_ref[...]
    home_rows = home.shape[0]
    low_hot = onehot(iota((128, entries), 0) == (wanted & 127))
    row_mask = iota((home_rows, entries), 0) == (wanted >> 7)
    owner_table = (home // blocks).astype(F32).astype(BF16)
    slot_table = (home % blocks).astype(F32).astype(BF16)

    def lookup(table):
        return jnp.sum(jnp.where(row_mask, dot(table, low_hot, NN), 0.0), axis=0, keepdims=True)

    owner = lookup(owner_table).astype(jnp.int32)
    slot = lookup(slot_table).astype(jnp.int32)
    member = iota((n, entries), 0) == owner
    earlier = onehot(iota((entries, entries), 0) < iota((entries, entries), 1))
    rank = jnp.sum(
        jnp.where(member, dot(onehot(member), earlier, NN), 0.0), axis=0, keepdims=True
    ).astype(jnp.int32)
    place_ref[...] = onehot(iota((slots, entries), 0) == owner * cap + rank)
    slot_hot = onehot(iota((blocks, entries), 0) == slot)
    ask_out[...] = dot(place_ref[...], slot_hot, NT).astype(BF16).reshape(n, cap, blocks)
    pl.semaphore_wait(barrier, n - 1)
    send_all((0, lambda d: ask_out.at[d], ask_in))
    ask_in[pl.ds(me, 1)] = ask_out[pl.ds(me, 1)]

    pieces = [quantize(p_ref[c]) for c in range(comps)]
    scales = exponent_lanes([e for _, _, e in pieces])

    everything(0, ask_in).wait_recv()
    asked = ask_in[...].reshape(slots, blocks)

    def place_words(selector, high, low):
        return (256.0 * dot(selector, high, NN) + dot(selector, low, NN)).astype(jnp.int32)

    shift = cap.bit_length() - 1
    in_group = iota((slots, 128), 0) & (cap - 1)
    spot = [iota((slots, 128), 1) == in_group + c * cap for c in range(comps)]
    of_device = onehot((iota((n, slots), 1) >> shift) == iota((n, slots), 0))
    device_of = onehot((iota((slots, n), 0) >> shift) == iota((slots, n), 1))

    def slot_scales(buffer):
        spread = dot(device_of, buffer[...].reshape(n, 128).astype(BF16), NN)
        return [
            jnp.exp2(jnp.sum(jnp.where(at, spread, 0.0), axis=1, keepdims=True) - 15.0)
            for at in spot
        ]

    def fill(buffer, scale_buffer, selector, quantized, scale_lanes):
        for c, (high, low, _) in enumerate(quantized):
            words = place_words(selector, high, low).astype(jnp.int16)
            buffer[:, :, c * pixels : (c + 1) * pixels] = words.reshape(n, cap, pixels)
        picked = dot(selector, scale_lanes, NN)
        row = jnp.zeros((slots, 128), F32)
        for c in range(comps):
            row = jnp.where(spot[c], picked[:, c : c + 1], row)
        scale_buffer[...] = dot(of_device, row.astype(BF16), NN).reshape(n, 1, 128)

    fill(ans_out, ans_scale_out, asked, pieces, scales)
    send_all(
        (3, lambda d: ans_scale_out.at[d], ans_scale_in),
        (1, lambda d: ans_out.at[d], ans_in),
    )
    ans_in[pl.ds(me, 1)] = ans_out[pl.ds(me, 1)]
    ans_scale_in[pl.ds(me, 1)] = ans_scale_out[pl.ds(me, 1)]

    for b in range(tblocks):
        for d in range(dets):
            here = slice(d * 128, (d + 1) * 128)
            pt_ref[b : b + 1, here] = point_ref[d : d + 1, b * 128 : (b + 1) * 128]
            cos_ref[b : b + 1, here] = angle_ref[d : d + 1, b * 128 : (b + 1) * 128]
    twice = 2.0 * cos_ref[...]
    cos_ref[...] = jnp.cos(twice)
    sin_ref[...] = jnp.sin(twice)

    def make_hot(b, c):
        pixel = pt_ref[pl.ds(b, 1), :] & (pixels - 1)
        hot_ref[b] = onehot(iota((pixels, wide), 0) == pixel)
        return c

    lax.fori_loop(0, tblocks, make_hot, 0)
    upper = iota((128, 128), 1) >= iota((128, 128), 0)

    def turned(tile):
        full = jnp.broadcast_to(tile.astype(F32), (128, 128))
        return pltpu.roll(full, 0, 1, stride=1, stride_axis=0)

    def make_toeplitz(b, before):
        lanes = pl.ds(pl.multiple_of(b * 128, 128), 128)
        now = []
        taps_here = filter_ref[:, lanes].astype(F32)
        for d in range(dets):
            tile = turned(taps_here[d : d + 1, :])
            toep_ref[d, :, lanes] = jnp.where(upper, tile, before[d]).astype(BF16)
            now.append(tile)
        return tuple(now)

    zero = jnp.zeros((128, 128), F32)
    last = lax.fori_loop(0, tap_rows, make_toeplitz, (zero,) * dets)
    for d in range(dets):
        toep_ref[d, :, taps : taps + 128] = jnp.where(upper, 0.0, last[d]).astype(BF16)

    everything(1, ans_in).wait_recv()
    everything(3, ans_scale_in).wait_recv()

    place = place_ref[...]
    scales_in = slot_scales(ans_scale_in)
    for c in range(comps):
        high, low = split(ans_in[:, :, c * pixels : (c + 1) * pixels].reshape(slots, pixels))
        scale = scales_in[c]
        lmh_ref[c] = dot(place, (high * (256.0 * scale)).astype(BF16), TN)
        lml_ref[c] = dot(place, (low * scale).astype(BF16), TN)

    def entry_mask(b):
        return iota((per_block, wide), 0) == (pt_ref[pl.ds(b, 1), :] // pixels)

    def scan_signal(b, carry):
        rows = pl.ds(pl.multiple_of(b * per_block, per_block), per_block)
        table = jnp.concatenate(
            [ref[c, rows, :] for c in range(comps) for ref in (lmh_ref, lml_ref)], axis=0
        ).astype(BF16)
        seen = dot(table, hot_ref[b], NN)
        parts = [
            seen[2 * c * per_block : (2 * c + 1) * per_block]
            + seen[(2 * c + 1) * per_block : (2 * c + 2) * per_block]
            for c in range(comps)
        ]
        value = (
            parts[0] + cos_ref[pl.ds(b, 1), :] * parts[1] + sin_ref[pl.ds(b, 1), :] * parts[2]
        )
        sig_ref[pl.ds(b, 1), :] = jnp.sum(
            jnp.where(entry_mask(b), value, 0.0), axis=0, keepdims=True
        )
        return carry

    lax.fori_loop(0, tblocks, scan_signal, 0, unroll=4)
    halo_out[...] = sig_ref[...].astype(BF16)

    def halo(side, target, buffer):
        return pltpu.make_async_remote_copy(
            src_ref=halo_out, dst_ref=buffer, send_sem=halo_send.at[side],
            recv_sem=halo_recv.at[side], device_id=(det, target),
            device_id_type=pl.DeviceIdType.MESH,
        )

    to_right = halo(0, (tm + 1) % n_tm, halo_low)
    to_left = halo(1, (tm + n_tm - 1) % n_tm, halo_high)

    @pl.when(tm < n_tm - 1)
    def _():
        to_right.start()

    @pl.when(tm > 0)
    def _():
        to_left.start()

    series_ref[tblocks : 2 * tblocks, :] = halo_out[...].astype(F32)

    @pl.when(tm > 0)
    def _():
        to_right.wait_recv()
        series_ref[0:tblocks, :] = halo_low[...].astype(F32)

    @pl.when(tm == 0)
    def _():
        series_ref[0:tblocks, :] = jnp.zeros((tblocks, wide), F32)

    @pl.when(tm < n_tm - 1)
    def _():
        to_left.wait_recv()
        series_ref[2 * tblocks : 3 * tblocks, :] = halo_high[...].astype(F32)

    @pl.when(tm == n_tm - 1)
    def _():
        series_ref[2 * tblocks : 3 * tblocks, :] = jnp.zeros((tblocks, wide), F32)

    def make_frames(group, c):
        near = series_ref[pl.ds(pl.multiple_of(group * 8, 8), tblocks + 8), :]
        for r in range(8):
            rows = near[r : r + tblocks, :].astype(BF16)
            lanes = pl.ds(pl.multiple_of((group * 8 + r) * 128, 128), 128)
            for d in range(dets):
                frames_ref[d, :, lanes] = rows[:, d * 128 : (d + 1) * 128]
        return c

    lax.fori_loop(0, tap_rows // 8, make_frames, 0)
    end = series_ref[2 * tblocks : 3 * tblocks, :].astype(BF16)
    for d in range(dets):
        frames_ref[d, :, taps : taps + 128] = end[:, d * 128 : (d + 1) * 128]
    for d in range(dets):
        y_ref[:, d * 128 : (d + 1) * 128] = (
            dot(frames_ref[d], toep_ref[d], NT).astype(BF16).astype(F32)
        )

    def scan_bins(b, carry):
        rows = pl.ds(pl.multiple_of(b * per_block, per_block), per_block)
        mask = entry_mask(b)
        filtered = y_ref[pl.ds(b, 1), :]
        stack = [jnp.where(mask, filtered, 0.0)]
        for weight in (cos_ref, sin_ref):
            term = jnp.where(mask, filtered * weight[pl.ds(b, 1), :], 0.0)
            high = term.astype(BF16).astype(F32)
            stack += [high, term - high]
        stack.append(jnp.zeros((per_block, wide), F32))
        sums = dot(jnp.concatenate(stack, axis=0).astype(BF16), hot_ref[b], NT)
        g = per_block
        part_ref[0, rows, :] = sums[0:g]
        part_ref[1, rows, :] = sums[g : 2 * g] + sums[2 * g : 3 * g]
        part_ref[2, rows, :] = sums[3 * g : 4 * g] + sums[4 * g : 5 * g]
        return carry

    lax.fori_loop(0, tblocks, scan_bins, 0, unroll=4)

    outgoing = [quantize(part_ref[c]) for c in range(comps)]
    fill(ret_out, ret_scale_out, place_ref[...], outgoing, exponent_lanes([e for _, _, e in outgoing]))
    send_all(
        (4, lambda d: ret_scale_out.at[d], ret_scale_in),
        (2, lambda d: ret_out.at[d], ret_in),
    )
    ret_in[pl.ds(me, 1)] = ret_out[pl.ds(me, 1)]
    ret_scale_in[pl.ds(me, 1)] = ret_scale_out[pl.ds(me, 1)]
    everything(2, ret_in).wait_recv()
    everything(4, ret_scale_in).wait_recv()

    chosen = ask_in[...].reshape(slots, blocks)
    scales_in = slot_scales(ret_scale_in)
    totals = [jnp.zeros((1, 1), F32)] * 4
    for c in range(comps):
        high, low = split(ret_in[:, :, c * pixels : (c + 1) * pixels].reshape(slots, pixels))
        scale = scales_in[c]
        image = dot(chosen, (high * (256.0 * scale)).astype(BF16), TN) + dot(
            chosen, (low * scale).astype(BF16), TN
        )
        image_ref[c] = image
        residual = r_ref[c]
        for i, product in enumerate(
            (residual * residual, p_ref[c] * image, residual * image, image * image)
        ):
            totals[i] = totals[i] + jnp.sum(product, keepdims=True)
    lane = iota((8, 128), 1)
    packed = jnp.zeros((8, 128), F32)
    for i in range(4):
        packed = jnp.where(lane == i, totals[i], packed)
    red_out[0] = packed

    def share(level, own, count, target):
        def copy(slot, peer):
            return pltpu.make_async_remote_copy(
                src_ref=red_out.at[level], dst_ref=red_in.at[level, slot],
                send_sem=red_send.at[level, peer], recv_sem=red_recv.at[level, slot],
                device_id=target(peer), device_id_type=pl.DeviceIdType.MESH,
            )

        for k in range(1, count):
            copy(own, (own + k) % count).start()
        red_in[level, pl.ds(own, 1)] = red_out[level].reshape(1, 8, 128)
        for k in range(1, count):
            peer = (own + count - k) % count
            copy(peer, peer).wait_recv()
        return jnp.sum(red_in[level, 0:count], axis=0), copy

    row_sum, row_copy = share(0, tm, n_tm, lambda peer: (det, peer))
    red_out[1] = row_sum
    full_sum, column_copy = share(1, det, n_det, lambda peer: (peer, tm))
    summed = full_sum[0:1, :]
    lane = iota((1, 128), 1)
    norm_old, curvature, cross, square = (
        jnp.sum(jnp.where(lane == i, summed, 0.0), axis=1, keepdims=True) for i in range(4)
    )
    step = norm_old / curvature
    norm_new = norm_old - 2.0 * step * cross + step * step * square
    ratio = norm_new / norm_old
    for c in range(comps):
        direction = p_ref[c]
        residual = r_ref[c] - step * image_ref[c]
        xo_ref[c] = x_ref[c] + step * direction
        ro_ref[c] = residual
        po_ref[c] = residual + ratio * direction

    everything(0, ask_out).wait_send()
    everything(1, ans_out).wait_send()
    everything(3, ans_scale_out).wait_send()
    everything(2, ret_out).wait_send()
    everything(4, ret_scale_out).wait_send()
    for copy, own, count in ((row_copy, tm, n_tm), (column_copy, det, n_det)):
        for k in range(1, count):
            copy(own, (own + k) % count).wait_send()

    @pl.when(tm < n_tm - 1)
    def _():
        to_right.wait_send()

    @pl.when(tm > 0)
    def _():
        to_left.wait_send()


def body(n_det, n_tm, x_map, r_map, p_map, pointing, pol_angle, noise_filter, block_list, block_home):
    n = n_det * n_tm
    comps, blocks, pixels = p_map.shape
    dets, samples = pointing.shape
    tblocks = block_list.shape[1]
    entries = tblocks * block_list.shape[2]
    taps = noise_filter.shape[1]
    cap = -(-(2 * entries // n) // 16) * 16
    slots = n * cap
    wide = dets * 128
    width = comps * pixels
    assert cap & (cap - 1) == 0 and 3 * cap <= 128
    assert samples == tblocks * 128 and taps == 2 * samples
    vmem = pltpu.VMEM
    out = jax.ShapeDtypeStruct(p_map.shape, F32)
    return pl.pallas_call(
        functools.partial(kernel, n_det, n_tm, cap),
        out_shape=(out, out, out),
        in_specs=[pl.BlockSpec(memory_space=vmem)] * 8,
        out_specs=[pl.BlockSpec(memory_space=vmem)] * 3,
        scratch_shapes=[
            vmem((n, cap, blocks), BF16),
            vmem((n, cap, blocks), BF16),
            vmem((n, cap, width), jnp.int16),
            vmem((n, cap, width), jnp.int16),
            vmem((n, cap, width), jnp.int16),
            vmem((n, cap, width), jnp.int16),
            vmem((2, 8, 128), F32),
            vmem((2, max(n_det, n_tm), 8, 128), F32),
            vmem((n, 1, 128), F32),
            vmem((n, 1, 128), F32),
            vmem((n, 1, 128), F32),
            vmem((n, 1, 128), F32),
            vmem((slots, entries), BF16),
            vmem((tblocks, pixels, wide), BF16),
            vmem((dets, 128, taps + 128), BF16),
            vmem((dets, tblocks, taps + 128), BF16),
            vmem((tblocks, wide), jnp.int32),
            vmem((tblocks, wide), F32),
            vmem((tblocks, wide), F32),
            vmem((tblocks, wide), F32),
            vmem((tblocks, wide), F32),
            vmem((3 * tblocks, wide), F32),
            vmem((tblocks, wide), BF16),
            vmem((tblocks, wide), BF16),
            vmem((tblocks, wide), BF16),
            vmem((comps, entries, pixels), F32),
            vmem((comps, entries, pixels), F32),
            vmem((comps, entries, pixels), F32),
            vmem((comps, blocks, pixels), F32),
            pltpu.SemaphoreType.DMA((5,)),
            pltpu.SemaphoreType.DMA((5,)),
            pltpu.SemaphoreType.DMA((2, max(n_det, n_tm))),
            pltpu.SemaphoreType.DMA((2, max(n_det, n_tm))),
            pltpu.SemaphoreType.DMA((2,)),
            pltpu.SemaphoreType.DMA((2,)),
        ],
        compiler_params=pltpu.CompilerParams(
            collective_id=0, has_side_effects=True, vmem_limit_bytes=60 * 1024 * 1024
        ),
    )(
        x_map, r_map, p_map, pointing, pol_angle, noise_filter,
        block_list.reshape(1, entries), block_home.reshape(-1, 128),
    )


def solution(mesh):
    maps = P(None, ("det", "tm"), None)
    return jax.shard_map(
        functools.partial(body, mesh.shape["det"], mesh.shape["tm"]),
        mesh=mesh,
        in_specs=(
            maps, maps, maps, P("det", "tm"), P("det", "tm"), P("det", None),
            P("det", "tm", None), P(),
        ),
        out_specs=(maps, maps, maps),
        check_vma=False,
    )
```

```python
import functools

import jax
import jax.numpy as jnp
from jax import lax
from jax.experimental import pallas as pl
from jax.experimental.pallas import tpu as pltpu
from jax.sharding import PartitionSpec as P

F32 = jnp.float32
BF16 = jnp.bfloat16
NN = (((1,), (0,)), ((), ()))
NT = (((1,), (1,)), ((), ()))
TN = (((0,), (0,)), ((), ()))


def dot(a, b, dims):
    return lax.dot_general(a, b, dims, preferred_element_type=F32)


def iota(shape, dim):
    return lax.broadcasted_iota(jnp.int32, shape, dim)


def onehot(cond):
    return jnp.where(cond, 1.0, 0.0).astype(BF16)


def quantize(value):
    largest = jnp.max(jnp.abs(value), axis=1, keepdims=True)
    exponent = jnp.ceil(jnp.log2(jnp.clip(largest, 1e-30, 1e30)))
    whole = jnp.clip(jnp.round(value * jnp.exp2(15.0 - exponent)), -32767.0, 32767.0)
    high = jnp.floor(whole * (1.0 / 256.0))
    return high.astype(BF16), (whole - 256.0 * high).astype(BF16), exponent


def split(words):
    whole = words.astype(jnp.int32).astype(F32)
    high = jnp.floor(whole * (1.0 / 256.0))
    return high, whole - 256.0 * high


def exponent_lanes(exponents):
    rows = exponents[0].shape[0]
    lane = iota((rows, 128), 1)
    out = jnp.zeros((rows, 128), F32)
    for c, e in enumerate(exponents):
        out = jnp.where(lane == c, e, out)
    return out.astype(BF16)


def kernel(
    n_det, n_tm, cap,
    x_ref, r_ref, p_ref, point_ref, angle_ref, filter_ref, wanted_ref, home_ref,
    xo_ref, ro_ref, po_ref,
    ask_out, ask_in, ans_out, ans_in, ret_out, ret_in, red_out, red_in,
    ans_scale_out, ans_scale_in, ret_scale_out, ret_scale_in,
    asked_ref, place_ref, hot_ref, toep_ref, frames_ref, pt_ref, cos_ref, sin_ref, sig_ref, y_ref,
    series_ref, halo_out, halo_low, halo_high, lmh_ref, lml_ref, part_ref, image_ref,
    send_sem, recv_sem, red_send, red_recv, halo_send, halo_recv,
):
    n = n_det * n_tm
    det, tm = lax.axis_index("det"), lax.axis_index("tm")
    me = det * n_tm + tm
    comps, blocks, pixels = p_ref.shape
    dets, samples = point_ref.shape
    entries = wanted_ref.shape[1]
    slots = n * cap
    tblocks = samples // 128
    per_block = entries // tblocks
    taps = filter_ref.shape[1]
    tap_rows = taps // 128
    half = n // 2
    wide = dets * 128

    def device(index):
        return (index // n_tm, index % n_tm)

    barrier = pltpu.get_barrier_semaphore()

    def greet(k, c):
        pl.semaphore_signal(
            barrier, inc=1, device_id=device((me + k) % n), device_id_type=pl.DeviceIdType.MESH
        )
        return c

    lax.fori_loop(1, n, greet, 0)

    def send_all(*sends):
        def start(peer):
            for stage, source, into in sends:
                pltpu.make_async_remote_copy(
                    src_ref=source(peer), dst_ref=into.at[me], send_sem=send_sem.at[stage],
                    recv_sem=recv_sem.at[stage], device_id=device(peer),
                    device_id_type=pl.DeviceIdType.MESH,
                ).start()

        mine = (me // half) * half

        def far(k, c):
            start((mine + half) % n + (me + k) % half)
            return c

        def near(k, c):
            start(mine + (me + k) % half)
            return c

        lax.fori_loop(0, half, far, 0)
        lax.fori_loop(1, half, near, 0)

    def everything(stage, buffer):
        whole = buffer.at[pl.ds(0, n - 1)]
        return pltpu.make_async_remote_copy(
            src_ref=whole, dst_ref=whole, send_sem=send_sem.at[stage],
            recv_sem=recv_sem.at[stage], device_id=device((me + 1) % n),
            device_id_type=pl.DeviceIdType.MESH,
        )

    wanted = wanted_ref[...]
    home = home_ref[...]
    home_rows = home.shape[0]
    low_hot = onehot(iota((128, entries), 0) == (wanted & 127))
    row_mask = iota((home_rows, entries), 0) == (wanted >> 7)
    owner_table = (home // blocks).astype(F32).astype(BF16)
    slot_table = (home % blocks).astype(F32).astype(BF16)

    def lookup(table):
        return jnp.sum(jnp.where(row_mask, dot(table, low_hot, NN), 0.0), axis=0, keepdims=True)

    owner = lookup(owner_table).astype(jnp.int32)
    slot = lookup(slot_table).astype(jnp.int32)
    member = iota((n, entries), 0) == owner
    earlier = onehot(iota((entries, entries), 0) < iota((entries, entries), 1))
    rank = jnp.sum(
        jnp.where(member, dot(onehot(member), earlier, NN), 0.0), axis=0, keepdims=True
    ).astype(jnp.int32)
    place_ref[...] = onehot(iota((slots, entries), 0) == owner * cap + rank)
    slot_hot = onehot(iota((blocks, entries), 0) == slot)
    shift = cap.bit_length() - 1
    in_group = iota((slots, 128), 0) & (cap - 1)
    spot = [iota((slots, 128), 1) == in_group + c * cap for c in range(comps)]
    of_device = onehot((iota((n, slots), 1) >> shift) == iota((n, slots), 0))
    device_of = onehot((iota((slots, n), 0) >> shift) == iota((slots, n), 1))
    named = dot(place_ref[...], slot_hot, NT) * (iota((slots, blocks), 1) + 1).astype(F32)
    named = jnp.where(spot[0], jnp.sum(named, axis=1, keepdims=True), 0.0).astype(BF16)
    ask_out[...] = dot(of_device, named, NN).reshape(n, 1, 128)
    pl.semaphore_wait(barrier, n - 1)
    send_all((0, lambda d: ask_out.at[d], ask_in))
    ask_in[pl.ds(me, 1)] = ask_out[pl.ds(me, 1)]

    pieces = [quantize(p_ref[c]) for c in range(comps)]
    scales = exponent_lanes([e for _, _, e in pieces])

    everything(0, ask_in).wait_recv()
    spread = dot(device_of, ask_in[...].reshape(n, 128).astype(BF16), NN)
    name = jnp.sum(jnp.where(spot[0], spread, 0.0), axis=1, keepdims=True).astype(jnp.int32)
    asked = onehot(iota((slots, blocks), 1) + 1 == name)
    asked_ref[...] = asked

    def place_words(selector, high, low):
        return (256.0 * dot(selector, high, NN) + dot(selector, low, NN)).astype(jnp.int32)

    def slot_scales(buffer):
        spread = dot(device_of, buffer[...].reshape(n, 128).astype(BF16), NN)
        return [
            jnp.exp2(jnp.sum(jnp.where(at, spread, 0.0), axis=1, keepdims=True) - 15.0)
            for at in spot
        ]

    def fill_and_send(out, into, scale_out, scale_in, stage, selector, quantized, scale_lanes):
        picked = dot(selector, scale_lanes, NN)
        row = jnp.zeros((slots, 128), F32)
        for c in range(comps):
            row = jnp.where(spot[c], picked[:, c : c + 1], row)
        scale_out[...] = dot(of_device, row.astype(BF16), NN).reshape(n, 1, 128)
        scale_in[pl.ds(me, 1)] = scale_out[pl.ds(me, 1)]
        sends = [(stage, lambda d: scale_out.at[d], scale_in)]
        for c, (high, low, _) in enumerate(quantized):
            words = place_words(selector, high, low).astype(jnp.int16)
            out[c] = words.reshape(n, cap, pixels)
            sends.append((stage + 1 + c, lambda d, c=c: out.at[c, d], into.at[c]))
            send_all(*sends)
            sends = []
            into[c, pl.ds(me, 1)] = out[c, pl.ds(me, 1)]

    fill_and_send(
        ans_out, ans_in, ans_scale_out, ans_scale_in, 1, asked, pieces, scales,
    )

    for b in range(tblocks):
        for d in range(dets):
            here = slice(d * 128, (d + 1) * 128)
            pt_ref[b : b + 1, here] = point_ref[d : d + 1, b * 128 : (b + 1) * 128]
            cos_ref[b : b + 1, here] = angle_ref[d : d + 1, b * 128 : (b + 1) * 128]
    twice = 2.0 * cos_ref[...]
    cos_ref[...] = jnp.cos(twice)
    sin_ref[...] = jnp.sin(twice)

    def make_hot(b, c):
        pixel = pt_ref[pl.ds(b, 1), :] & (pixels - 1)
        hot_ref[b] = onehot(iota((pixels, wide), 0) == pixel)
        return c

    lax.fori_loop(0, tblocks, make_hot, 0)
    upper = iota((128, 128), 1) >= iota((128, 128), 0)

    def turned(tile):
        full = jnp.broadcast_to(tile.astype(F32), (128, 128))
        return pltpu.roll(full, 0, 1, stride=1, stride_axis=0)

    def make_toeplitz(b, before):
        lanes = pl.ds(pl.multiple_of(b * 128, 128), 128)
        now = []
        taps_here = filter_ref[:, lanes].astype(F32)
        for d in range(dets):
            tile = turned(taps_here[d : d + 1, :])
            toep_ref[d, :, lanes] = jnp.where(upper, tile, before[d]).astype(BF16)
            now.append(tile)
        return tuple(now)

    zero = jnp.zeros((128, 128), F32)
    last = lax.fori_loop(0, tap_rows, make_toeplitz, (zero,) * dets)
    for d in range(dets):
        toep_ref[d, :, taps : taps + 128] = jnp.where(upper, 0.0, last[d]).astype(BF16)

    everything(1, ans_scale_in).wait_recv()

    place = place_ref[...]
    scales_in = slot_scales(ans_scale_in)
    for c in range(comps):
        everything(1 + 1 + c, ans_in.at[c]).wait_recv()
        high, low = split(ans_in[c].reshape(slots, pixels))
        scale = scales_in[c]
        lmh_ref[c] = dot(place, (high * (256.0 * scale)).astype(BF16), TN)
        lml_ref[c] = dot(place, (low * scale).astype(BF16), TN)

    def entry_mask(b):
        return iota((per_block, wide), 0) == (pt_ref[pl.ds(b, 1), :] // pixels)

    def scan_signal(b, carry):
        rows = pl.ds(pl.multiple_of(b * per_block, per_block), per_block)
        table = jnp.concatenate(
            [ref[c, rows, :] for c in range(comps) for ref in (lmh_ref, lml_ref)], axis=0
        ).astype(BF16)
        seen = dot(table, hot_ref[b], NN)
        parts = [
            seen[2 * c * per_block : (2 * c + 1) * per_block]
            + seen[(2 * c + 1) * per_block : (2 * c + 2) * per_block]
            for c in range(comps)
        ]
        value = (
            parts[0] + cos_ref[pl.ds(b, 1), :] * parts[1] + sin_ref[pl.ds(b, 1), :] * parts[2]
        )
        sig_ref[pl.ds(b, 1), :] = jnp.sum(
            jnp.where(entry_mask(b), value, 0.0), axis=0, keepdims=True
        )
        return carry

    lax.fori_loop(0, tblocks, scan_signal, 0, unroll=4)
    halo_out[...] = sig_ref[...].astype(BF16)

    def halo(side, target, buffer):
        return pltpu.make_async_remote_copy(
            src_ref=halo_out, dst_ref=buffer, send_sem=halo_send.at[side],
            recv_sem=halo_recv.at[side], device_id=(det, target),
            device_id_type=pl.DeviceIdType.MESH,
        )

    to_right = halo(0, (tm + 1) % n_tm, halo_low)
    to_left = halo(1, (tm + n_tm - 1) % n_tm, halo_high)

    @pl.when(tm < n_tm - 1)
    def _():
        to_right.start()

    @pl.when(tm > 0)
    def _():
        to_left.start()

    series_ref[tblocks : 2 * tblocks, :] = halo_out[...].astype(F32)

    @pl.when(tm > 0)
    def _():
        to_right.wait_recv()
        series_ref[0:tblocks, :] = halo_low[...].astype(F32)

    @pl.when(tm == 0)
    def _():
        series_ref[0:tblocks, :] = jnp.zeros((tblocks, wide), F32)

    @pl.when(tm < n_tm - 1)
    def _():
        to_left.wait_recv()
        series_ref[2 * tblocks : 3 * tblocks, :] = halo_high[...].astype(F32)

    @pl.when(tm == n_tm - 1)
    def _():
        series_ref[2 * tblocks : 3 * tblocks, :] = jnp.zeros((tblocks, wide), F32)

    def make_frames(group, c):
        near = series_ref[pl.ds(pl.multiple_of(group * 8, 8), tblocks + 8), :]
        for r in range(8):
            rows = near[r : r + tblocks, :].astype(BF16)
            lanes = pl.ds(pl.multiple_of((group * 8 + r) * 128, 128), 128)
            for d in range(dets):
                frames_ref[d, :, lanes] = rows[:, d * 128 : (d + 1) * 128]
        return c

    lax.fori_loop(0, tap_rows // 8, make_frames, 0)
    end = series_ref[2 * tblocks : 3 * tblocks, :].astype(BF16)
    for d in range(dets):
        frames_ref[d, :, taps : taps + 128] = end[:, d * 128 : (d + 1) * 128]
    for d in range(dets):
        y_ref[:, d * 128 : (d + 1) * 128] = (
            dot(frames_ref[d], toep_ref[d], NT).astype(BF16).astype(F32)
        )

    def scan_bins(b, carry):
        rows = pl.ds(pl.multiple_of(b * per_block, per_block), per_block)
        mask = entry_mask(b)
        filtered = y_ref[pl.ds(b, 1), :]
        stack = [jnp.where(mask, filtered, 0.0)]
        for weight in (cos_ref, sin_ref):
            term = jnp.where(mask, filtered * weight[pl.ds(b, 1), :], 0.0)
            high = term.astype(BF16).astype(F32)
            stack += [high, term - high]
        stack.append(jnp.zeros((per_block, wide), F32))
        sums = dot(jnp.concatenate(stack, axis=0).astype(BF16), hot_ref[b], NT)
        g = per_block
        part_ref[0, rows, :] = sums[0:g]
        part_ref[1, rows, :] = sums[g : 2 * g] + sums[2 * g : 3 * g]
        part_ref[2, rows, :] = sums[3 * g : 4 * g] + sums[4 * g : 5 * g]
        return carry

    lax.fori_loop(0, tblocks, scan_bins, 0, unroll=4)

    outgoing = [quantize(part_ref[c]) for c in range(comps)]
    fill_and_send(
        ret_out, ret_in, ret_scale_out, ret_scale_in, 5, place_ref[...], outgoing,
        exponent_lanes([e for _, _, e in outgoing]),
    )
    everything(5, ret_scale_in).wait_recv()

    chosen = asked_ref[...]
    scales_in = slot_scales(ret_scale_in)
    totals = [jnp.zeros((1, 1), F32)] * 4
    for c in range(comps):
        everything(5 + 1 + c, ret_in.at[c]).wait_recv()
        high, low = split(ret_in[c].reshape(slots, pixels))
        scale = scales_in[c]
        image = dot(chosen, (high * (256.0 * scale)).astype(BF16), TN) + dot(
            chosen, (low * scale).astype(BF16), TN
        )
        image_ref[c] = image
        residual = r_ref[c]
        for i, product in enumerate(
            (residual * residual, p_ref[c] * image, residual * image, image * image)
        ):
            totals[i] = totals[i] + jnp.sum(product, keepdims=True)
    lane = iota((8, 128), 1)
    packed = jnp.zeros((8, 128), F32)
    for i in range(4):
        packed = jnp.where(lane == i, totals[i], packed)
    red_out[0] = packed

    def share(level, own, count, target):
        def copy(slot, peer):
            return pltpu.make_async_remote_copy(
                src_ref=red_out.at[level], dst_ref=red_in.at[level, slot],
                send_sem=red_send.at[level, peer], recv_sem=red_recv.at[level, slot],
                device_id=target(peer), device_id_type=pl.DeviceIdType.MESH,
            )

        for k in range(1, count):
            copy(own, (own + k) % count).start()
        red_in[level, pl.ds(own, 1)] = red_out[level].reshape(1, 8, 128)
        for k in range(1, count):
            peer = (own + count - k) % count
            copy(peer, peer).wait_recv()
        return jnp.sum(red_in[level, 0:count], axis=0), copy

    row_sum, row_copy = share(0, tm, n_tm, lambda peer: (det, peer))
    red_out[1] = row_sum
    full_sum, column_copy = share(1, det, n_det, lambda peer: (peer, tm))
    summed = full_sum[0:1, :]
    lane = iota((1, 128), 1)
    norm_old, curvature, cross, square = (
        jnp.sum(jnp.where(lane == i, summed, 0.0), axis=1, keepdims=True) for i in range(4)
    )
    step = norm_old / curvature
    norm_new = norm_old - 2.0 * step * cross + step * step * square
    ratio = norm_new / norm_old
    for c in range(comps):
        direction = p_ref[c]
        residual = r_ref[c] - step * image_ref[c]
        xo_ref[c] = x_ref[c] + step * direction
        ro_ref[c] = residual
        po_ref[c] = residual + ratio * direction

    everything(0, ask_out).wait_send()
    for c in range(comps):
        everything(1 + 1 + c, ans_out.at[c]).wait_send()
    everything(1, ans_scale_out).wait_send()
    for c in range(comps):
        everything(5 + 1 + c, ret_out.at[c]).wait_send()
    everything(5, ret_scale_out).wait_send()
    for copy, own, count in ((row_copy, tm, n_tm), (column_copy, det, n_det)):
        for k in range(1, count):
            copy(own, (own + k) % count).wait_send()

    @pl.when(tm < n_tm - 1)
    def _():
        to_right.wait_send()

    @pl.when(tm > 0)
    def _():
        to_left.wait_send()


def body(n_det, n_tm, x_map, r_map, p_map, pointing, pol_angle, noise_filter, block_list, block_home):
    n = n_det * n_tm
    comps, blocks, pixels = p_map.shape
    dets, samples = pointing.shape
    tblocks = block_list.shape[1]
    entries = tblocks * block_list.shape[2]
    taps = noise_filter.shape[1]
    cap = -(-(2 * entries // n) // 16) * 16
    slots = n * cap
    wide = dets * 128
    assert cap & (cap - 1) == 0 and 3 * cap <= 128 and blocks < 256
    assert samples == tblocks * 128 and taps == 2 * samples
    vmem = pltpu.VMEM
    out = jax.ShapeDtypeStruct(p_map.shape, F32)
    return pl.pallas_call(
        functools.partial(kernel, n_det, n_tm, cap),
        out_shape=(out, out, out),
        in_specs=[pl.BlockSpec(memory_space=vmem)] * 8,
        out_specs=[pl.BlockSpec(memory_space=vmem)] * 3,
        scratch_shapes=[
            vmem((n, 1, 128), F32),
            vmem((n, 1, 128), F32),
            vmem((comps, n, cap, pixels), jnp.int16),
            vmem((comps, n, cap, pixels), jnp.int16),
            vmem((comps, n, cap, pixels), jnp.int16),
            vmem((comps, n, cap, pixels), jnp.int16),
            vmem((2, 8, 128), F32),
            vmem((2, max(n_det, n_tm), 8, 128), F32),
            vmem((n, 1, 128), F32),
            vmem((n, 1, 128), F32),
            vmem((n, 1, 128), F32),
            vmem((n, 1, 128), F32),
            vmem((slots, blocks), BF16),
            vmem((slots, entries), BF16),
            vmem((tblocks, pixels, wide), BF16),
            vmem((dets, 128, taps + 128), BF16),
            vmem((dets, tblocks, taps + 128), BF16),
            vmem((tblocks, wide), jnp.int32),
            vmem((tblocks, wide), F32),
            vmem((tblocks, wide), F32),
            vmem((tblocks, wide), F32),
            vmem((tblocks, wide), F32),
            vmem((3 * tblocks, wide), F32),
            vmem((tblocks, wide), BF16),
            vmem((tblocks, wide), BF16),
            vmem((tblocks, wide), BF16),
            vmem((comps, entries, pixels), F32),
            vmem((comps, entries, pixels), F32),
            vmem((comps, entries, pixels), F32),
            vmem((comps, blocks, pixels), F32),
            pltpu.SemaphoreType.DMA((9,)),
            pltpu.SemaphoreType.DMA((9,)),
            pltpu.SemaphoreType.DMA((2, max(n_det, n_tm))),
            pltpu.SemaphoreType.DMA((2, max(n_det, n_tm))),
            pltpu.SemaphoreType.DMA((2,)),
            pltpu.SemaphoreType.DMA((2,)),
        ],
        compiler_params=pltpu.CompilerParams(
            collective_id=0, has_side_effects=True, vmem_limit_bytes=60 * 1024 * 1024
        ),
    )(
        x_map, r_map, p_map, pointing, pol_angle, noise_filter,
        block_list.reshape(1, entries), block_home.reshape(-1, 128),
    )


def solution(mesh):
    maps = P(None, ("det", "tm"), None)
    return jax.shard_map(
        functools.partial(body, mesh.shape["det"], mesh.shape["tm"]),
        mesh=mesh,
        in_specs=(
            maps, maps, maps, P("det", "tm"), P("det", "tm"), P("det", None),
            P("det", "tm", None), P(),
        ),
        out_specs=(maps, maps, maps),
        check_vma=False,
    )
```
